512 devices in a mesh: row: 16 (over z), col: 8 (over x, core), leaf: 4 (over y).
Axes of the slice: x: 4, y: 4, z: 16, core: 2. Of those that a mesh axis runs over, the one named last changes fastest.
Arguments:
- leaf_rhs: bfloat16 [4, 2, 512, 4096], P('leaf', None, 'col', 'row'), may hold values from -6 to 6
- root_rhs: bfloat16 [2, 512, 4096], P(None, 'col', 'row'), may hold values from -6 to 6
- leaf_lower: bfloat16 [4, 1, 4096, 4096], P('leaf', None, 'row', 'col'), may hold values from -0.046875 to 0.046875
- leaf_coupling_lower: bfloat16 [4, 2, 2, 4096, 4096], P('leaf', None, None, 'row', 'col'), may hold values from -0.046875 to 0.046875
- root_lower: bfloat16 [1, 4096, 4096], P(None, 'row', 'col'), may hold values from -0.046875 to 0.046875
- leaf_upper: bfloat16 [4, 1, 4096, 4096], P('leaf', None, 'row', 'col'), may hold values from -0.046875 to 0.046875
- leaf_coupling_upper: bfloat16 [4, 2, 2, 4096, 4096], P('leaf', None, None, 'row', 'col'), may hold values from -0.046875 to 0.046875
- root_upper: bfloat16 [1, 4096, 4096], P(None, 'row', 'col'), may hold values from -0.046875 to 0.046875
- leaf_lower_inv: float32 [4, 2, 32, 128, 128], P('leaf', None, 'row'), may hold values from -1 to 2, as said below
- root_lower_inv: float32 [2, 32, 128, 128], P(None, 'row'), may hold values from -1 to 2, as said below
- leaf_upper_inv: float32 [4, 2, 32, 128, 128], P('leaf', None, 'row'), may hold values from -1 to 2, as said below
- root_upper_inv: float32 [2, 32, 128, 128], P(None, 'row'), may hold values from -1 to 2, as said below
Outputs:
- leaf_solution: bfloat16 [4, 2, 512, 4096], P('leaf', None, 'col', 'row')
- root_solution: bfloat16 [2, 512, 4096], P(None, 'col', 'row')
The draws below stay inside these ranges and needn't reach their ends.
Inputs may be any that keep to these rules, and one draw needn't show every extreme that they name: `leaf_lower_inv`: each 128 x 128 matrix is lower triangular with unit diagonal. `root_lower_inv`: each 128 x 128 matrix is lower triangular with unit diagonal. `leaf_upper_inv`: each 128 x 128 matrix is upper triangular with a positive diagonal. `root_upper_inv`: each 128 x 128 matrix is upper triangular with a positive diagonal.
All inputs are finite; a program needn't handle non-finite values.
Results may differ from the reference program's by a relative error of at most 0.03.
Values may be sent and summed in bfloat16 or wider, within the bound.
A program may use at most 64 MiB of HBM per device.

```python
import jax
import jax.numpy as jnp
from jax import lax

W = 128
RHS = 512
LEV_S = 2
LEV_R = 2
SN = 32
NL = 4096
PL = 1
PR = 1
N_LEAF = 4


def triangle(values_raw, diagonal_values, lower):
    block_width = values_raw.shape[-1]
    row_ids = lax.broadcasted_iota(jnp.int32, (block_width, block_width), 0)
    col_ids = lax.broadcasted_iota(jnp.int32, (block_width, block_width), 1)
    if lower:
        strict_mask = row_ids > col_ids
    else:
        strict_mask = row_ids < col_ids
    diagonal_mask = row_ids == col_ids
    return jnp.where(strict_mask, values_raw, 0.0) + jnp.where(diagonal_mask, diagonal_values[..., :, None], 0.0)


def draw_leaf_lower_inv(key, part):
    key = jax.random.fold_in(key, 11)
    array_shape = (N_LEAF, LEV_S, SN, W, W)
    values_raw = jax.random.truncated_normal(key, -4.0, 4.0, array_shape, jnp.float32) * 0.5 * W ** (-0.5)
    return triangle(values_raw, jnp.ones(array_shape[:-1], jnp.float32), True)


def draw_root_lower_inv(key, part):
    key = jax.random.fold_in(key, 17)
    array_shape = (LEV_R, SN, W, W)
    values_raw = jax.random.truncated_normal(key, -4.0, 4.0, array_shape, jnp.float32) * 0.5 * W ** (-0.5)
    return triangle(values_raw, jnp.ones(array_shape[:-1], jnp.float32), True)


def draw_leaf_upper_inv(key, part):
    key = jax.random.fold_in(key, 13)
    first, second = jax.random.split(key)
    array_shape = (N_LEAF, LEV_S, SN, W, W)
    values_raw = jax.random.truncated_normal(first, -4.0, 4.0, array_shape, jnp.float32) * 0.5 * W ** (-0.5)
    diagonal_values = jnp.exp(jax.random.uniform(second, array_shape[:-1], jnp.float32, -0.69, 0.69))
    return triangle(values_raw, diagonal_values, False)


def draw_root_upper_inv(key, part):
    key = jax.random.fold_in(key, 19)
    first, second = jax.random.split(key)
    array_shape = (LEV_R, SN, W, W)
    values_raw = jax.random.truncated_normal(first, -4.0, 4.0, array_shape, jnp.float32) * 0.5 * W ** (-0.5)
    diagonal_values = jnp.exp(jax.random.uniform(second, array_shape[:-1], jnp.float32, -0.69, 0.69))
    return triangle(values_raw, diagonal_values, False)


def steps_of(own_key, dims, cuts, low, top_value):
    loudness = 1.0
    for axis_at, blocks in cuts:
        draws = jax.random.uniform(jax.random.fold_in(jax.random.fold_in(own_key, 6), axis_at), (blocks,), jnp.float32, low / len(cuts), top_value / len(cuts))
        loudness = loudness * jnp.repeat(jnp.exp(draws), dims[axis_at] // blocks).reshape((-1,) + (1,) * (len(dims) - 1 - axis_at))
    return loudness


def normal_values(key, extent, scale, reach, cuts=(), kind=jnp.bfloat16):
    level = steps_of(key, extent, cuts, -0.22, 0.18) if cuts else 1.0
    values = jax.random.normal(key, extent, jnp.float32) * scale * level
    return jnp.minimum(jnp.maximum(values, -reach), reach).astype(kind)


def setup_inputs(seed: int = 0) -> dict:
    splits = jax.random.split(jax.random.key(seed), 13)
    leaf_rhs = normal_values(splits[0], (N_LEAF, LEV_S, RHS, NL), 1.0, 6.0, ((0, 4), (2, 8), (3, 16)))
    root_rhs = normal_values(splits[1], (LEV_R, RHS, NL), 1.0, 6.0, ((1, 8), (2, 16)))
    leaf_lower = normal_values(splits[2], (N_LEAF, PL, NL, NL), (4 * NL) ** -0.5, 0.046875, ((0, 4), (2, 16), (3, 8)))
    leaf_coupling_lower = normal_values(splits[3], (N_LEAF, LEV_R, LEV_S, NL, NL), (4 * NL) ** -0.5, 0.046875, ((0, 4), (3, 16), (4, 8)))
    root_lower = normal_values(splits[4], (PR, NL, NL), (4 * NL) ** -0.5, 0.046875, ((1, 16), (2, 8)))
    leaf_upper = normal_values(splits[5], (N_LEAF, PL, NL, NL), (4 * NL) ** -0.5, 0.046875, ((0, 4), (2, 16), (3, 8)))
    leaf_coupling_upper = normal_values(splits[6], (N_LEAF, LEV_S, LEV_R, NL, NL), (4 * NL) ** -0.5, 0.046875, ((0, 4), (3, 16), (4, 8)))
    root_upper = normal_values(splits[7], (PR, NL, NL), (4 * NL) ** -0.5, 0.046875, ((1, 16), (2, 8)))
    leaf_lower_inv = draw_leaf_lower_inv(jax.random.fold_in(splits[12], 71), 0)
    root_lower_inv = draw_root_lower_inv(jax.random.fold_in(splits[12], 71), 0)
    leaf_upper_inv = draw_leaf_upper_inv(jax.random.fold_in(splits[12], 71), 0)
    root_upper_inv = draw_root_upper_inv(jax.random.fold_in(splits[12], 71), 0)
    return {"leaf_rhs": leaf_rhs, "root_rhs": root_rhs, "leaf_lower": leaf_lower, "leaf_coupling_lower": leaf_coupling_lower, "root_lower": root_lower, "leaf_upper": leaf_upper, "leaf_coupling_upper": leaf_coupling_upper, "root_upper": root_upper, "leaf_lower_inv": leaf_lower_inv, "root_lower_inv": root_lower_inv, "leaf_upper_inv": leaf_upper_inv, "root_upper_inv": root_upper_inv}


def pair_index(high, low):
    return high * (high - 1) // 2 + low


def multiply(vector, block):
    return lax.dot_general(vector, block, (((1,), (1,)), ((), ())), preferred_element_type=jnp.float32)


def solve_block(inverse, right_side):
    rhs_count = right_side.shape[0]
    blocks = inverse.shape[0]
    block_width = inverse.shape[1]
    blocked = right_side.reshape(rhs_count, blocks, block_width)
    result = jnp.einsum("sab,qsb->qsa", inverse, blocked, precision=lax.Precision.HIGHEST)
    return result.reshape(rhs_count, blocks * block_width).astype(jnp.bfloat16)


def reference(leaf_rhs, root_rhs, leaf_lower, leaf_coupling_lower, root_lower, leaf_upper, leaf_coupling_upper, root_upper, leaf_lower_inv, root_lower_inv, leaf_upper_inv, root_upper_inv):
    leaf_y = []
    ancestor = [jnp.zeros((RHS, NL), jnp.float32) for m in range(LEV_R)]
    for replica in range(N_LEAF):
        level_y = []
        for k in range(LEV_S):
            right_side = leaf_rhs[replica, k].astype(jnp.float32)
            for j in range(k):
                right_side = right_side - multiply(level_y[j], leaf_lower[replica, pair_index(k, j)])
            level_y.append(solve_block(leaf_lower_inv[replica, k], right_side))
        for m in range(LEV_R):
            for j in range(LEV_S):
                ancestor[m] = ancestor[m] + multiply(level_y[j], leaf_coupling_lower[replica, m, j])
        leaf_y.append(level_y)
    root_y = []
    for m in range(LEV_R):
        right_side = root_rhs[m].astype(jnp.float32) - ancestor[m]
        for i in range(m):
            right_side = right_side - multiply(root_y[i], root_lower[pair_index(m, i)])
        root_y.append(solve_block(root_lower_inv[m], right_side))
    root_x = [None] * LEV_R
    for m in reversed(range(LEV_R)):
        right_side = root_y[m].astype(jnp.float32)
        for i in range(m + 1, LEV_R):
            right_side = right_side - multiply(root_x[i], root_upper[pair_index(i, m)])
        root_x[m] = solve_block(root_upper_inv[m], right_side)
    leaf_x = []
    for replica in range(N_LEAF):
        level_x = [None] * LEV_S
        for k in reversed(range(LEV_S)):
            right_side = leaf_y[replica][k].astype(jnp.float32)
            for j in range(k + 1, LEV_S):
                right_side = right_side - multiply(level_x[j], leaf_upper[replica, pair_index(j, k)])
            for m in range(LEV_R):
                right_side = right_side - multiply(root_x[m], leaf_coupling_upper[replica, k, m])
            level_x[k] = solve_block(leaf_upper_inv[replica, k], right_side)
        leaf_x.append(jnp.stack(level_x))
    return jnp.stack(leaf_x), jnp.stack(root_x)
```

```python
import jax
import jax.numpy as jnp
from jax import lax
from jax.experimental import pallas as pl
from jax.experimental.pallas import tpu as pltpu
from jax.sharding import PartitionSpec as P

MESH = pl.DeviceIdType.MESH
H = 2
LH = 4 // H
R = 64 // H
BF = jnp.bfloat16
F32 = jnp.float32
NEAR = [(2, 0), (2, 1), (1, 0), (1, 1), (3, 0), (3, 1), (0, 1)]
N_SEM = 256


def dot_t(a, b):
    return lax.dot_general(a, b, (((1,), (1,)), ((), ())), preferred_element_type=F32)


def solve(inverse, right):
    parts = []
    for s in range(2):
        parts.append(
            lax.dot_general(
                right[:, 128 * s : 128 * (s + 1)],
                inverse[s],
                (((1,), (1,)), ((), ())),
                preferred_element_type=F32,
                precision=lax.Precision.HIGHEST,
            )
        )
    return jnp.concatenate(parts, axis=1).astype(BF)


def kernel(
    leaf_rhs,
    root_rhs,
    leaf_lower,
    coupling_lower,
    root_lower,
    leaf_upper,
    coupling_upper,
    root_upper,
    leaf_lower_inv,
    root_lower_inv,
    leaf_upper_inv,
    root_upper_inv,
    leaf_out,
    root_out,
    b_leaf,
    b_root,
    w_ll,
    w_cl,
    w_rl,
    w_lu,
    w_cu,
    w_ru,
    i_ll,
    i_rl,
    i_lu,
    i_ru,
    yb,
    wb,
    zb,
    xb,
    base1,
    v_y,
    v_w,
    v_z,
    v_x,
    p_y,
    p_a,
    p_w,
    p_r,
    s_y,
    s_a,
    s_w,
    s_r,
    r_y,
    r_a,
    r_w,
    r_r,
    ro,
    sems,
):
    z = lax.axis_index("row")
    c = lax.axis_index("col")
    l = lax.axis_index("leaf")
    x = lax.div(c, 2)
    core = lax.rem(c, 2)
    ct = lax.div(z, 2)
    hl = lax.div(l, LH)
    lt = pl.multiple_of(lax.rem(l, LH) * 16, 16)
    taken = [0]

    def sem():
        taken[0] += 1
        return sems.at[taken[0] - 1]

    def zed(d):
        return lax.rem(z + (d + 32), 16)

    def plane(d):
        return lax.rem(l + (d + 8), 4)

    def colm(dx, dc):
        return lax.rem(x + (dx + 4), 4) * 2 + lax.rem(core + dc, 2)

    def await_bytes(ref, s):
        pltpu.make_async_copy(ref, ref, s).wait()

    sent = []

    def send(src, dst, send_sem, recv_sem, where):
        copy = pltpu.make_async_remote_copy(
            src_ref=src, dst_ref=dst, send_sem=send_sem, recv_sem=recv_sem, device_id=where, device_id_type=MESH
        )
        copy.start()
        return copy

    def load(pairs):
        copies = []
        for src, dst in pairs:
            copy = pltpu.make_async_copy(src, dst, sem())
            copy.start()
            copies.append(copy)

        def done():
            for copy in copies:
                copy.wait()

        return done

    def halves(src, dst):
        return [(src.at[:, pl.ds(256 * b, 256)], dst.at[b]) for b in range(2)]

    first_load = load([(leaf_rhs.at[0], b_leaf), (leaf_lower_inv.at[0], i_ll)])
    load_ll = load(halves(leaf_lower.at[0, 0], w_ll))
    pairs = [(root_rhs, b_root), (root_lower_inv, i_rl), (leaf_upper_inv.at[0], i_lu), (root_upper_inv, i_ru)]
    for m in range(2):
        for j in range(2):
            pairs += halves(coupling_lower.at[0, m, j], w_cl.at[m, j])
            pairs += halves(coupling_upper.at[0, m, j], w_cu.at[m, j])
    pairs += halves(root_lower.at[0], w_rl)
    pairs += halves(leaf_upper.at[0, 0], w_lu)
    pairs += halves(root_upper.at[0], w_ru)
    load_rest = load(pairs)

    barrier = pltpu.get_barrier_semaphore()

    def greet(where):
        pl.semaphore_signal(barrier, inc=1, device_id=where, device_id_type=MESH)

    greeted = 0
    for b in range(2):
        for k in range(8):
            greet((2 * c + b, k, l))
            greeted += 1
    for dy in range(4):
        for dx, dc in NEAR + [(0, 0)]:
            if (dy, dx, dc) != (0, 0, 0):
                greet((z, colm(dx, dc), plane(dy)))
                greeted += 1
    for d in (-2, -1, 1):
        greet((zed(d), c, l))
        greeted += 1

    p_y[...] = jnp.zeros_like(p_y)
    p_a[...] = jnp.zeros_like(p_a)
    p_w[...] = jnp.zeros_like(p_w)

    def spread_far(src, v):
        s_one, s_rest, r = sem(), sem(), sem()
        kind = 2 * lax.rem(z, 2) + lax.div(c, 4)
        off = lax.rem(kind - z + 16, 4)
        dst = v.at[lax.rem(z, 2), c]
        for i in (2, 1, 3):
            send(src, dst, s_rest, r, (zed(off + 4 * i), ct, l))
        first = zed(off)
        me = (first == z) & (ct == c)

        @pl.when(me)
        def _():
            pltpu.make_async_copy(src, dst, r).start()

        @pl.when(jnp.logical_not(me))
        def _():
            send(src, dst, s_one, r, (first, ct, l))

        def finish():
            await_bytes(v.at[0, pl.ds(0, 3)], s_rest)

            @pl.when(jnp.logical_not(me))
            def _():
                await_bytes(src, s_one)

        sent.append(finish)
        return lambda: await_bytes(v.at[0, pl.ds(0, 4)], r)

    def class_of(d):
        j = lax.rem(z + (d + 16), 4)
        return lax.div(j, 2), lax.rem(j, 2) * 4

    def spread_near(v):
        b, first = class_of(0)
        block = v.at[b, pl.ds(first, 4)]
        s = sem()
        waits = []
        for d in (2, 1, -1):
            r = sem()
            send(block, block, s, r, (zed(d), c, l))
            waits.append((-d, r))

        sent.append(lambda: await_bytes(v.at[:, pl.ds(0, 6)], s))

        def arrivals():
            for d, r in (waits[1], waits[2], waits[0]):
                await_bytes(block, r)
                yield d

        return arrivals

    def add_class(acc, v, w, d):
        b, first = class_of(d)
        rows = v[b, pl.ds(first, 4)].reshape(4 * R, 256)
        acc[pl.ds(first, 4)] += dot_t(rows, w[b]).reshape(4, R, 256)

    def add_all(acc, v, w):
        total = dot_t(v[0].reshape(8 * R, 256), w[0]) + dot_t(v[1].reshape(8 * R, 256), w[1])
        acc[...] += total.reshape(8, R, 256)

    def reduce_start(p, s_ref, r_ref):
        s, r = sem(), sem()
        s_ref[...] = p[...].astype(BF)
        for i, (dx, dc) in enumerate(NEAR):
            other = colm(dx, dc)
            send(s_ref.at[other], r_ref.at[i], s, r, (z, other, l))
        sent.append(lambda: await_bytes(r_ref, s))

        def result():
            await_bytes(r_ref, r)
            total = p[c]
            for i in range(7):
                total = total + r_ref[i].astype(F32)
            return total

        return result

    a_recv = [sem(), sem()]

    def reduce_leaf_start(m, h):
        s_ref = s_a.at[m, h]
        s_ref[...] = p_a[m, h].astype(BF)
        s = sem()
        for dx, dc in NEAR + [(0, 0)]:
            for t in range(LH):
                there = h * LH + t
                other = colm(dx, dc)
                k = (NEAR + [(0, 0)]).index((dx, dc))
                slot = lax.rem(l - there + 4, 4)
                src = s_ref.at[other, pl.ds(16 * t, 16)]
                dst = r_a.at[m, 4 * k + slot - (k == 7)]
                if (dx, dc) == (0, 0):
                    own = sem()
                    away = l != there

                    @pl.when(away)
                    def _():
                        send(src, dst, own, a_recv[m], (z, other, there))

                    def finish(away=away, own=own, src=src):
                        @pl.when(away)
                        def _():
                            await_bytes(src, own)

                    sent.append(finish)
                else:
                    send(src, dst, s, a_recv[m], (z, other, there))
        sent.append(lambda: await_bytes(s_ref.at[pl.ds(0, 7)], s))

    def reduce_leaf_result(m):
        await_bytes(r_a.at[m], a_recv[m])
        total = p_a[m, hl, c, pl.ds(lt, 16)]
        for slot in range(31):
            total = total + r_a[m, slot].astype(F32)
        return total

    def spread_root(src, dst):
        s_one, s_rest, r = sem(), sem(), sem()
        for d in (8, 7, 9, 6, 10, 5, 11, 4, 12, 3, 13, 2, 14, 1, 15):
            send(src, dst, s_rest, r, (zed(d), ct, l))
        me = ct == c

        @pl.when(me)
        def _():
            pltpu.make_async_copy(src, dst, r).start()

        @pl.when(jnp.logical_not(me))
        def _():
            send(src, dst, s_one, r, (z, ct, l))

        def finish():
            await_bytes(r_a.at[0, pl.ds(0, 15)], s_rest)

            @pl.when(jnp.logical_not(me))
            def _():
                await_bytes(src, s_one)

        sent.append(finish)
        return lambda: await_bytes(v_z, r)

    def multiply_root(get, w, p):
        total = dot_t(get(0).reshape(128, 256), w[0]) + dot_t(get(1).reshape(128, 256), w[1])
        p[...] = total.reshape(8, 16, 256)

    lower_b = lambda k, h: b_leaf[k, pl.ds(R * h, R)].astype(F32)

    pl.semaphore_wait(barrier, greeted)
    first_load()

    def lower(h):
        yb[0, h] = solve(i_ll.at[0], lower_b(0, h))
        far = spread_far(yb.at[0, h], v_y.at[0, h])
        if h == 0:
            load_ll()
        yield
        far()
        near = spread_near(v_y.at[0, h])
        add_class(p_y.at[h], v_y.at[0, h], w_ll, 0)
        yield
        for d in near():
            add_class(p_y.at[h], v_y.at[0, h], w_ll, d)
        total = reduce_start(p_y.at[h], s_y.at[h], r_y.at[h])
        if h == 0:
            load_rest()
        for m in range(2):
            add_all(p_a.at[m, h], v_y.at[0, h], w_cl.at[m, 0])
        yield
        yb[1, h] = solve(i_ll.at[1], lower_b(1, h) - total())
        far = spread_far(yb.at[1, h], v_y.at[1, h])
        yield
        far()
        near = spread_near(v_y.at[1, h])
        add_class(p_a.at[0, h], v_y.at[1, h], w_cl.at[0, 1], 0)
        yield
        for d in near():
            add_class(p_a.at[0, h], v_y.at[1, h], w_cl.at[0, 1], d)
        reduce_leaf_start(0, h)
        yield
        add_all(p_a.at[1, h], v_y.at[1, h], w_cl.at[1, 1])
        reduce_leaf_start(1, h)

    gathered = {}

    def x_part(m):
        return v_x.at[m, hl, :, :, pl.ds(lt, 16), :]

    def gather_send(m):
        send_sems = [sem() for _ in range(3)]
        first = taken[0]
        taken[0] += 4
        for i, d in enumerate((2, 1, 3)):
            send(x_part(m), x_part(m), send_sems[i], sems.at[first + (4 - d)], (z, c, plane(d)))
            sent.append(lambda s=send_sems[i]: await_bytes(v_z, s))
        gathered[m] = first

    def gather_wait(m, h):
        for t in range(LH):
            there = h * LH + t
            d = lax.rem(there - l + 4, 4)

            @pl.when(d != 0)
            def _():
                await_bytes(v_z, sems.at[gathered[m] + d])

    out_first = {}

    def out_send(m):
        first = taken[0]
        taken[0] += 4
        ro[m, l] = xb[m]
        for d in (2, 1, 3):
            s = sem()
            send(xb.at[m], ro.at[m, l], s, sems.at[first + (4 - d)], (z, c, plane(d)))
            sent.append(lambda s=s: await_bytes(xb.at[m], s))
        out_first[m] = first

    def out_wait(m):
        for d in (1, 2, 3):
            await_bytes(xb.at[m], sems.at[out_first[m] + d])

    def root():
        rows = pl.ds(pl.multiple_of(l * 16, 16), 16)
        zb[0] = solve(i_rl.at[0], b_root[0, rows].astype(F32) - reduce_leaf_result(0))
        done = spread_root(zb.at[0], v_z.at[lax.rem(z, 2), c])
        base1[...] = b_root[1, rows].astype(F32) - reduce_leaf_result(1)
        done()
        multiply_root(lambda b: v_z[b], w_rl, p_r.at[0])
        total = reduce_start(p_r.at[0], s_r.at[0], r_r.at[0])
        z1 = solve(i_rl.at[1], base1[...] - total())
        xb[1] = solve(i_ru.at[1], z1.astype(F32))
        done = spread_root(xb.at[1], v_x.at[1, hl, lax.rem(z, 2), c, pl.ds(lt, 16)])
        out_send(1)
        done()
        gather_send(1)
        multiply_root(lambda b: v_x[1, hl, b, :, pl.ds(lt, 16), :], w_ru, p_r.at[1])
        total = reduce_start(p_r.at[1], s_r.at[1], r_r.at[1])
        xb[0] = solve(i_ru.at[0], zb[0].astype(F32) - total())
        done = spread_root(xb.at[0], v_x.at[0, hl, lax.rem(z, 2), c, pl.ds(lt, 16)])
        out_send(0)
        for h in range(H):
            gather_wait(1, h)
            for k in (1, 0):
                add_all(p_w.at[k, h], v_x.at[1, h], w_cu.at[k, 1])
        done()
        gather_send(0)

    def upper(h):
        gather_wait(0, h)
        add_all(p_w.at[1, h], v_x.at[0, h], w_cu.at[1, 0])
        total = reduce_start(p_w.at[1, h], s_w.at[1, h], r_w.at[1, h])
        add_all(p_w.at[0, h], v_x.at[0, h], w_cu.at[0, 0])
        yield
        wb[h] = solve(i_lu.at[1], yb[1, h].astype(F32) - total())
        far = spread_far(wb.at[h], v_w.at[h])
        leaf_out[0, 1, pl.ds(R * h, R)] = wb[h]
        yield
        far()
        near = spread_near(v_w.at[h])
        add_class(p_w.at[0, h], v_w.at[h], w_lu, 0)
        yield
        for d in near():
            add_class(p_w.at[0, h], v_w.at[h], w_lu, d)
        total = reduce_start(p_w.at[0, h], s_w.at[0, h], r_w.at[0, h])
        yield
        leaf_out[0, 0, pl.ds(R * h, R)] = solve(i_lu.at[0], yb[0, h].astype(F32) - total())

    def in_turn(chains):
        chains = list(chains)
        while chains:
            chains = [chain for chain in chains if next(chain, chain) is not chain]

    in_turn([lower(h) for h in range(H)])
    root()
    in_turn([upper(h) for h in range(H)])
    for m in range(2):
        out_wait(m)
        root_out[m] = ro[m].reshape(64, 256)
    for finish in sent:
        finish()


def on_device(*args):
    vmem = pltpu.VMEM
    scratch = [
        vmem((2, 64, 256), BF),
        vmem((2, 64, 256), BF),
        vmem((2, 256, 256), BF),
        vmem((2, 2, 2, 256, 256), BF),
        vmem((2, 256, 256), BF),
        vmem((2, 256, 256), BF),
        vmem((2, 2, 2, 256, 256), BF),
        vmem((2, 256, 256), BF),
        vmem((2, 2, 128, 128), F32),
        vmem((2, 2, 128, 128), F32),
        vmem((2, 2, 128, 128), F32),
        vmem((2, 2, 128, 128), F32),
        vmem((2, H, R, 256), BF),
        vmem((H, R, 256), BF),
        vmem((2, 16, 256), BF),
        vmem((2, 16, 256), BF),
        vmem((16, 256), F32),
        vmem((2, H, 2, 8, R, 256), BF),
        vmem((H, 2, 8, R, 256), BF),
        vmem((2, 8, 16, 256), BF),
        vmem((2, H, 2, 8, R, 256), BF),
        vmem((H, 8, R, 256), F32),
        vmem((2, H, 8, R, 256), F32),
        vmem((2, H, 8, R, 256), F32),
        vmem((2, 8, 16, 256), F32),
        vmem((H, 8, R, 256), BF),
        vmem((2, H, 8, R, 256), BF),
        vmem((2, H, 8, R, 256), BF),
        vmem((2, 8, 16, 256), BF),
        vmem((H, 7, R, 256), BF),
        vmem((2, 31, 16, 256), BF),
        vmem((2, H, 7, R, 256), BF),
        vmem((2, 7, 16, 256), BF),
        vmem((2, 4, 16, 256), BF),
        pltpu.SemaphoreType.DMA((N_SEM,)),
    ]
    return pl.pallas_call(
        kernel,
        out_shape=(
            jax.ShapeDtypeStruct((1, 2, 64, 256), BF),
            jax.ShapeDtypeStruct((2, 64, 256), BF),
        ),
        in_specs=[pl.BlockSpec(memory_space=pl.ANY)] * 12,
        out_specs=(pl.BlockSpec(memory_space=pltpu.VMEM),) * 2,
        scratch_shapes=scratch,
        compiler_params=pltpu.CompilerParams(
            collective_id=0, has_side_effects=True, vmem_limit_bytes=48 * 2**20
        ),
    )(*args)


def solution(mesh):
    placed = (
        P("leaf", None, "col", "row"),
        P(None, "col", "row"),
        P("leaf", None, "row", "col"),
        P("leaf", None, None, "row", "col"),
        P(None, "row", "col"),
        P("leaf", None, "row", "col"),
        P("leaf", None, None, "row", "col"),
        P(None, "row", "col"),
        P("leaf", None, "row", None, None),
        P(None, "row", None, None),
        P("leaf", None, "row", None, None),
        P(None, "row", None, None),
    )
    return jax.shard_map(
        on_device,
        mesh=mesh,
        in_specs=placed,
        out_specs=(P("leaf", None, "col", "row"), P(None, "col", "row")),
        check_vma=False,
    )
```

```python
import jax
import jax.numpy as jnp
from jax import lax
from jax.experimental import pallas as pl
from jax.experimental.pallas import tpu as pltpu
from jax.sharding import PartitionSpec as P

MESH = pl.DeviceIdType.MESH
H = 4
TURNS = (0, 1, 3, 2)
ORDER = (0, 0, 1, 3, 2, 0, 1, 3, 2, 0, 1, 3, 2, 0, 1, 3, 2, 1, 3, 2)
R = 64 // H
BF = jnp.bfloat16
F32 = jnp.float32
NEAR = [(2, 0), (2, 1), (1, 0), (1, 1), (3, 0), (3, 1), (0, 1)]
N_SEM = 88


def dot_t(a, b):
    return lax.dot_general(a, b, (((1,), (1,)), ((), ())), preferred_element_type=F32)


def solve(inverse, right):
    parts = []
    for s in range(2):
        parts.append(
            lax.dot_general(
                right[:, 128 * s : 128 * (s + 1)],
                inverse[s],
                (((1,), (1,)), ((), ())),
                preferred_element_type=F32,
                precision=lax.Precision.HIGHEST,
            )
        )
    return jnp.concatenate(parts, axis=1).astype(BF)


def kernel(
    leaf_rhs,
    root_rhs,
    leaf_lower,
    coupling_lower,
    root_lower,
    leaf_upper,
    coupling_upper,
    root_upper,
    leaf_lower_inv,
    root_lower_inv,
    leaf_upper_inv,
    root_upper_inv,
    leaf_out,
    root_out,
    b_leaf,
    b_root,
    w_ll,
    w_cl,
    w_rl,
    w_lu,
    w_cu,
    w_ru,
    i_ll,
    i_rl,
    i_lu,
    i_ru,
    yb,
    wb,
    zb,
    xb,
    base1,
    v_y,
    v_w,
    v_z,
    v_x,
    p_y,
    p_a,
    p_w,
    p_r,
    s_y,
    s_a,
    s_w,
    s_r,
    r_y,
    r_a,
    r_w,
    r_r,
    ro,
    spare,
    bytes_of,
    sems,
):
    z = lax.axis_index("row")
    c = lax.axis_index("col")
    l = lax.axis_index("leaf")
    x = lax.div(c, 2)
    core = lax.rem(c, 2)
    ct = lax.div(z, 2)
    taken = [0]

    def sem():
        taken[0] += 1
        return sems.at[taken[0] - 1]

    def zed(d):
        return lax.rem(z + (d + 32), 16)

    def plane(d):
        return lax.rem(l + (d + 8), 4)

    def colm(dx, dc):
        return lax.rem(x + (dx + 4), 4) * 2 + lax.rem(core + dc, 2)

    def await_bytes(ref, s):
        pltpu.make_async_copy(ref, ref, s).wait()

    gone = sem()
    units = [0, 0]

    def size(ref):
        total = 1
        for n in ref.shape:
            total *= n
        return total // 4096

    def send(src, dst, recv_sem, where):
        units[0] += size(src)
        pltpu.make_async_remote_copy(
            src_ref=src, dst_ref=dst, send_sem=gone, recv_sem=recv_sem, device_id=where, device_id_type=MESH
        ).start()

    def send_unless(me, src, dst, recv_sem, where):
        unused = spare.at[units[1]]
        units[1] += 1

        @pl.when(me)
        def _():
            if dst is not None:
                pltpu.make_async_copy(src, dst, recv_sem).start()
            pltpu.make_async_copy(src, unused, gone).start()

        @pl.when(jnp.logical_not(me))
        def _():
            send(src, where[0], recv_sem, where[1])

    def load(pairs):
        s, total = sem(), 0
        for src, dst in pairs:
            pltpu.make_async_copy(src, dst, s).start()
            total += size(dst) * (2 if dst.dtype == F32 else 1)
        return lambda: await_bytes(bytes_of.at[pl.ds(0, total)], s)

    def halves(src, dst):
        return [(src.at[:, pl.ds(256 * b, 256)], dst.at[b]) for b in range(2)]

    barrier = pltpu.get_barrier_semaphore()

    def greet(where):
        pl.semaphore_signal(barrier, inc=1, device_id=where, device_id_type=MESH)

    greeted = 0
    for b in range(2):
        for k in range(8):
            greet((2 * c + b, k, l))
            greeted += 1
    for dy in range(4):
        for dx, dc in NEAR + [(0, 0)]:
            if (dy, dx, dc) != (0, 0, 0):
                greet((z, colm(dx, dc), plane(dy)))
                greeted += 1
    for d in (-2, -1, 1, 2):
        greet((zed(d), c, l))
        greeted += 1

    first_load = load([(leaf_rhs.at[0], b_leaf), (leaf_lower_inv.at[0], i_ll)])
    load_ll = load(halves(leaf_lower.at[0, 0], w_ll))
    pairs = [(root_rhs, b_root), (root_lower_inv, i_rl), (leaf_upper_inv.at[0], i_lu), (root_upper_inv, i_ru)]
    for m in range(2):
        for j in range(2):
            pairs += halves(coupling_lower.at[0, m, j], w_cl.at[m, j])
            pairs += halves(coupling_upper.at[0, m, j], w_cu.at[m, j])
    pairs += halves(root_lower.at[0], w_rl)
    pairs += halves(leaf_upper.at[0, 0], w_lu)
    pairs += halves(root_upper.at[0], w_ru)
    load_rest = load(pairs)

    p_y[...] = jnp.zeros_like(p_y)
    p_a[...] = jnp.zeros_like(p_a)
    p_w[...] = jnp.zeros_like(p_w)

    def spread_far(src, v):
        r = sem()
        kind = 2 * lax.rem(z, 2) + lax.div(c, 4)
        off = lax.rem(kind - z + 16, 4)
        dst = v.at[lax.rem(z, 2), c]
        for i in (2, 1, 3):
            send(src, dst, r, (zed(off + 4 * i), ct, l))
        first = zed(off)
        me = (first == z) & (ct == c)
        send_unless(me, src, dst, r, (dst, (first, ct, l)))
        return lambda: await_bytes(v.at[0, pl.ds(0, 4)], r)

    def class_of(d):
        j = lax.rem(z + (d + 16), 4)
        return lax.div(j, 2), lax.rem(j, 2) * 4

    def spread_near(v):
        b, first = class_of(0)
        block = v.at[b, pl.ds(first, 4)]
        parts = [v.at[b, pl.ds(first, 2)], v.at[b, pl.ds(first + 2, 2)]]
        r_next, r_prev, r_far = sem(), sem(), sem()
        send(block, block, r_next, (zed(1), c, l))
        send(block, block, r_prev, (zed(-1), c, l))
        send(parts[0], parts[0], r_far, (zed(2), c, l))
        send(parts[1], parts[1], r_far, (zed(-2), c, l))

        def arrivals():
            for d, r in ((-1, r_next), (1, r_prev), (2, r_far)):
                await_bytes(block, r)
                yield d

        return arrivals

    def add_class(acc, v, w, d):
        b, first = class_of(d)
        rows = v[b, pl.ds(first, 4)].reshape(4 * R, 256)
        acc[pl.ds(first, 4)] += dot_t(rows, w[b]).reshape(4, R, 256)

    def add_all(acc, v, w):
        total = dot_t(v[0].reshape(8 * R, 256), w[0]) + dot_t(v[1].reshape(8 * R, 256), w[1])
        acc[...] += total.reshape(8, R, 256)

    def reduce_start(p, s_ref, r_ref):
        r = sem()
        s_ref[...] = p[...].astype(BF)
        for i, (dx, dc) in enumerate(NEAR):
            other = colm(dx, dc)
            send(s_ref.at[other], r_ref.at[i], r, (z, other, l))

        def result():
            await_bytes(r_ref, r)
            total = p[c]
            for i in range(7):
                total = total + r_ref[i].astype(F32)
            return total

        return result

    a_recv = [sem(), sem()]

    def reduce_leaf_start(m, h):
        s_ref = s_a.at[m, h]
        s_ref[...] = p_a[m, h].astype(BF)
        slot = lax.rem(l - h + 4, 4)
        for k, (dx, dc) in enumerate(NEAR + [(0, 0)]):
            other = colm(dx, dc)
            if k < 7:
                send(s_ref.at[other], r_a.at[m, 4 * k + slot], a_recv[m], (z, other, h))
            else:
                there = (r_a.at[m, 27 + slot], (z, other, h))
                send_unless(l == h, s_ref.at[other], None, a_recv[m], there)

    def reduce_leaf_result(m):
        await_bytes(r_a.at[m], a_recv[m])
        total = p_a[m, l, c]
        for slot in range(31):
            total = total + r_a[m, slot].astype(F32)
        return total

    def spread_root(src, dst):
        r = sem()
        for d in (8, 7, 9, 6, 10, 5, 11, 4, 12, 3, 13, 2, 14, 1, 15):
            send(src, dst, r, (zed(d), ct, l))
        send_unless(ct == c, src, dst, r, (dst, (z, ct, l)))
        return lambda: await_bytes(v_z, r)

    def multiply_root(get, w, p):
        total = dot_t(get(0).reshape(128, 256), w[0]) + dot_t(get(1).reshape(128, 256), w[1])
        p[...] = total.reshape(8, 16, 256)

    lower_b = lambda k, h: b_leaf[k, pl.ds(R * h, R)].astype(F32)

    pl.semaphore_wait(barrier, greeted)
    first_load()

    def lower(h):
        yb[0, h] = solve(i_ll.at[0], lower_b(0, h))
        far = spread_far(yb.at[0, h], v_y.at[0, h])
        if h == 0:
            load_ll()
        yield
        far()
        near = spread_near(v_y.at[0, h])
        add_class(p_y.at[h], v_y.at[0, h], w_ll, 0)
        yield
        for d in near():
            add_class(p_y.at[h], v_y.at[0, h], w_ll, d)
        total = reduce_start(p_y.at[h], s_y.at[h], r_y.at[h])
        if h == 0:
            load_rest()
        for m in range(2):
            add_all(p_a.at[m, h], v_y.at[0, h], w_cl.at[m, 0])
        yield
        yb[1, h] = solve(i_ll.at[1], lower_b(1, h) - total())
        far = spread_far(yb.at[1, h], v_y.at[1, h])
        yield
        far()
        near = spread_near(v_y.at[1, h])
        add_class(p_a.at[0, h], v_y.at[1, h], w_cl.at[0, 1], 0)
        yield
        for d in near():
            add_class(p_a.at[0, h], v_y.at[1, h], w_cl.at[0, 1], d)
        reduce_leaf_start(0, h)
        yield
        add_all(p_a.at[1, h], v_y.at[1, h], w_cl.at[1, 1])
        reduce_leaf_start(1, h)

    gathered = {}

    def gather_send(m):
        gathered[m] = [None] + [sem() for _ in range(3)]
        for d in (2, 1, 3):
            send(v_x.at[m, l], v_x.at[m, l], gathered[m][4 - d], (z, c, plane(d)))

    def gather_wait(m, t):
        if t:
            await_bytes(v_z, gathered[m][t])

    ro_recv = sem()

    def out_send(m):
        ro[m, l] = xb[m]
        for d in (2, 1, 3):
            send(xb.at[m], ro.at[m, l], ro_recv, (z, c, plane(d)))

    def root():
        rows = pl.ds(pl.multiple_of(l * 16, 16), 16)
        zb[0] = solve(i_rl.at[0], b_root[0, rows].astype(F32) - reduce_leaf_result(0))
        done = spread_root(zb.at[0], v_z.at[lax.rem(z, 2), c])
        base1[...] = b_root[1, rows].astype(F32) - reduce_leaf_result(1)
        done()
        multiply_root(lambda b: v_z[b], w_rl, p_r.at[0])
        total = reduce_start(p_r.at[0], s_r.at[0], r_r.at[0])
        z1 = solve(i_rl.at[1], base1[...] - total())
        xb[1] = solve(i_ru.at[1], z1.astype(F32))
        done = spread_root(xb.at[1], v_x.at[1, l, lax.rem(z, 2), c])
        out_send(1)
        done()
        gather_send(1)
        multiply_root(lambda b: v_x[1, l, b], w_ru, p_r.at[1])
        total = reduce_start(p_r.at[1], s_r.at[1], r_r.at[1])
        xb[0] = solve(i_ru.at[0], zb[0].astype(F32) - total())
        done = spread_root(xb.at[0], v_x.at[0, l, lax.rem(z, 2), c])
        out_send(0)
        for t in TURNS:
            gather_wait(1, t)
            for k in (1, 0):
                add_all(p_w.at[k, t], v_x.at[1, plane(t)], w_cu.at[k, 1])
        done()
        gather_send(0)

    def upper(t):
        h = plane(t)
        rows = pl.ds(pl.multiple_of(h * R, R), R)
        gather_wait(0, t)
        add_all(p_w.at[1, t], v_x.at[0, h], w_cu.at[1, 0])
        total = reduce_start(p_w.at[1, t], s_w.at[1, t], r_w.at[1, t])
        add_all(p_w.at[0, t], v_x.at[0, h], w_cu.at[0, 0])
        yield
        wb[t] = solve(i_lu.at[1], yb[1, h].astype(F32) - total())
        far = spread_far(wb.at[t], v_w.at[t])
        leaf_out[0, 1, rows] = wb[t]
        yield
        far()
        near = spread_near(v_w.at[t])
        add_class(p_w.at[0, t], v_w.at[t], w_lu, 0)
        yield
        for d in near():
            add_class(p_w.at[0, t], v_w.at[t], w_lu, d)
        total = reduce_start(p_w.at[0, t], s_w.at[0, t], r_w.at[0, t])
        yield
        leaf_out[0, 0, rows] = solve(i_lu.at[0], yb[0, h].astype(F32) - total())

    def in_turn(chains):
        chains = list(chains)
        while chains:
            chains = [chain for chain in chains if next(chain, chain) is not chain]

    in_turn([lower(h) for h in range(H)])
    root()
    chains = [upper(t) for t in range(4)]
    for t in ORDER:
        next(chains[t], None)
    await_bytes(bytes_of.at[pl.ds(0, 6)], ro_recv)
    for m in range(2):
        root_out[m] = ro[m].reshape(64, 256)
    await_bytes(bytes_of.at[pl.ds(0, units[0])], gone)


def on_device(*args):
    vmem = pltpu.VMEM
    scratch = [
        vmem((2, 64, 256), BF),
        vmem((2, 64, 256), BF),
        vmem((2, 256, 256), BF),
        vmem((2, 2, 2, 256, 256), BF),
        vmem((2, 256, 256), BF),
        vmem((2, 256, 256), BF),
        vmem((2, 2, 2, 256, 256), BF),
        vmem((2, 256, 256), BF),
        vmem((2, 2, 128, 128), F32),
        vmem((2, 2, 128, 128), F32),
        vmem((2, 2, 128, 128), F32),
        vmem((2, 2, 128, 128), F32),
        vmem((2, H, R, 256), BF),
        vmem((H, R, 256), BF),
        vmem((2, 16, 256), BF),
        vmem((2, 16, 256), BF),
        vmem((16, 256), F32),
        vmem((2, H, 2, 8, R, 256), BF),
        vmem((H, 2, 8, R, 256), BF),
        vmem((2, 8, 16, 256), BF),
        vmem((2, H, 2, 8, R, 256), BF),
        vmem((H, 8, R, 256), F32),
        vmem((2, H, 8, R, 256), F32),
        vmem((2, H, 8, R, 256), F32),
        vmem((2, 8, 16, 256), F32),
        vmem((H, 8, R, 256), BF),
        vmem((2, H, 8, R, 256), BF),
        vmem((2, H, 8, R, 256), BF),
        vmem((2, 8, 16, 256), BF),
        vmem((H, 7, R, 256), BF),
        vmem((2, 31, 16, 256), BF),
        vmem((2, H, 7, R, 256), BF),
        vmem((2, 7, 16, 256), BF),
        vmem((2, 4, 16, 256), BF),
        vmem((24, 16, 256), BF),
        vmem((1024, 16, 256), BF),
        pltpu.SemaphoreType.DMA((N_SEM,)),
    ]
    return pl.pallas_call(
        kernel,
        out_shape=(
            jax.ShapeDtypeStruct((1, 2, 64, 256), BF),
            jax.ShapeDtypeStruct((2, 64, 256), BF),
        ),
        in_specs=[pl.BlockSpec(memory_space=pl.ANY)] * 12,
        out_specs=(pl.BlockSpec(memory_space=pltpu.VMEM),) * 2,
        scratch_shapes=scratch,
        compiler_params=pltpu.CompilerParams(
            collective_id=0, has_side_effects=True, vmem_limit_bytes=63 * 2**20
        ),
    )(*args)


def solution(mesh):
    placed = (
        P("leaf", None, "col", "row"),
        P(None, "col", "row"),
        P("leaf", None, "row", "col"),
        P("leaf", None, None, "row", "col"),
        P(None, "row", "col"),
        P("leaf", None, "row", "col"),
        P("leaf", None, None, "row", "col"),
        P(None, "row", "col"),
        P("leaf", None, "row", None, None),
        P(None, "row", None, None),
        P("leaf", None, "row", None, None),
        P(None, "row", None, None),
    )
    return jax.shard_map(
        on_device,
        mesh=mesh,
        in_specs=placed,
        out_specs=(P("leaf", None, "col", "row"), P(None, "col", "row")),
        check_vma=False,
    )
```

```python
import jax
import jax.numpy as jnp
from jax import lax
from jax.experimental import pallas as pl
from jax.experimental.pallas import tpu as pltpu
from jax.sharding import PartitionSpec as P

MESH = pl.DeviceIdType.MESH
H = 4
TURNS = (0, 1, 3, 2)
ORDER = (0, 0, 0, 1, 3, 2, 1, 3, 2, 0, 1, 3, 2, 0, 1, 3, 2, 0, 1, 3, 2, 1, 3, 2)
R = 64 // H
BF = jnp.bfloat16
F32 = jnp.float32
NEAR = [(2, 0), (2, 1), (1, 0), (1, 1), (3, 0), (3, 1), (0, 1)]
N_SEM = 54


def dot_t(a, b):
    return lax.dot_general(a, b, (((1,), (1,)), ((), ())), preferred_element_type=F32)


def solve(inverse, right):
    parts = []
    for s in range(2):
        parts.append(
            lax.dot_general(
                right[:, 128 * s : 128 * (s + 1)],
                inverse[s],
                (((1,), (1,)), ((), ())),
                preferred_element_type=F32,
                precision=lax.Precision.HIGHEST,
            )
        )
    return jnp.concatenate(parts, axis=1).astype(BF)


def kernel(
    leaf_rhs,
    root_rhs,
    leaf_lower,
    coupling_lower,
    root_lower,
    leaf_upper,
    coupling_upper,
    root_upper,
    leaf_lower_inv,
    root_lower_inv,
    leaf_upper_inv,
    root_upper_inv,
    leaf_out,
    root_out,
    b_leaf,
    b_root,
    w_ll,
    w_cl,
    w_rl,
    w_lu,
    w_cu,
    w_ru,
    i_ll,
    i_rl,
    i_lu,
    i_ru,
    yb,
    wb,
    zb,
    xb,
    base1,
    v_y,
    v_w,
    v_z,
    v_x,
    p_y,
    p_a,
    p_w,
    p_r,
    s_y,
    s_a,
    s_w,
    s_r,
    r_y,
    r_a,
    r_w,
    r_r,
    ro,
    spare,
    bytes_of,
    i_both,
    sems,
):
    z = lax.axis_index("row")
    c = lax.axis_index("col")
    l = lax.axis_index("leaf")
    x = lax.div(c, 2)
    core = lax.rem(c, 2)
    ct = lax.div(z, 2)
    taken = [0]

    def sem():
        taken[0] += 1
        return sems.at[taken[0] - 1]

    def zed(d):
        return lax.rem(z + (d + 32), 16)

    def plane(d):
        return lax.rem(l + (d + 8), 4)

    def colm(dx, dc):
        return lax.rem(x + (dx + 4), 4) * 2 + lax.rem(core + dc, 2)

    def await_bytes(ref, s):
        pltpu.make_async_copy(ref, ref, s).wait()

    gone = sem()
    units = [0, 0]

    def size(ref):
        total = 1
        for n in ref.shape:
            total *= n
        return total // 4096

    def send(src, dst, recv_sem, where):
        units[0] += size(src)
        pltpu.make_async_remote_copy(
            src_ref=src, dst_ref=dst, send_sem=gone, recv_sem=recv_sem, device_id=where, device_id_type=MESH
        ).start()

    def send_unless(me, src, dst, recv_sem, where):
        unused = spare.at[units[1]]
        units[1] += 1

        @pl.when(me)
        def _():
            if dst is not None:
                pltpu.make_async_copy(src, dst, recv_sem).start()
            pltpu.make_async_copy(src, unused, gone).start()

        @pl.when(jnp.logical_not(me))
        def _():
            send(src, where[0], recv_sem, where[1])

    def load(pairs):
        s, total = sem(), 0
        for src, dst in pairs:
            pltpu.make_async_copy(src, dst, s).start()
            total += size(dst) * (2 if dst.dtype == F32 else 1)
        return lambda: await_bytes(bytes_of.at[pl.ds(0, total)], s)

    def halves(src, dst):
        return [(src.at[:, pl.ds(256 * b, 256)], dst.at[b]) for b in range(2)]

    barrier = pltpu.get_barrier_semaphore()

    def greet(where):
        pl.semaphore_signal(barrier, inc=1, device_id=where, device_id_type=MESH)

    greeted = 0
    for b in range(2):
        for k in range(8):
            greet((2 * c + b, k, l))
            greeted += 1
    for dy in range(4):
        for dx, dc in NEAR + [(0, 0)]:
            if (dy, dx, dc) != (0, 0, 0):
                greet((z, colm(dx, dc), plane(dy)))
                greeted += 1
    for d in (-2, -1, 1, 2):
        greet((zed(d), c, l))
        greeted += 1

    first_load = load([(leaf_rhs.at[0], b_leaf), (leaf_lower_inv.at[0], i_ll)])
    load_ll = load(halves(leaf_lower.at[0, 0], w_ll))
    pairs = [(root_rhs, b_root), (root_lower_inv, i_rl), (leaf_upper_inv.at[0], i_lu), (root_upper_inv, i_ru)]
    for m in range(2):
        for j in range(2):
            pairs += halves(coupling_lower.at[0, m, j], w_cl.at[m, j])
            pairs += halves(coupling_upper.at[0, m, j], w_cu.at[m, j])
    pairs += halves(root_lower.at[0], w_rl)
    pairs += halves(leaf_upper.at[0, 0], w_lu)
    pairs += halves(root_upper.at[0], w_ru)
    load_rest = load(pairs)

    p_y[...] = jnp.zeros_like(p_y)
    p_a[...] = jnp.zeros_like(p_a)
    p_w[...] = jnp.zeros_like(p_w)

    def spread_far(src, v):
        r = sem()
        off = 1 + lax.rem(z, 2) + lax.div(c, 4)
        dst = v.at[lax.rem(z, 2), c]
        for i in (2, 1, 3, 0):
            send(src, dst, r, (zed(off + 4 * i), ct, l))
        return lambda: await_bytes(v.at[0, pl.ds(0, 4)], r)

    def spread_near(v):
        j = lax.rem(z - 2 * c + 31, 4)
        b, first = lax.div(j, 2), lax.rem(j, 2) * 4
        block = v.at[b, pl.ds(first, 4)]
        parts = [v.at[b, pl.ds(first, 2)], v.at[b, pl.ds(first + 2, 2)]]
        r = sem()
        send(parts[0], parts[0], r, (zed(2), c, l))
        send(parts[1], parts[1], r, (zed(-2), c, l))
        send(block, block, r, (zed(1), c, l))
        send(block, block, r, (zed(-1), c, l))
        return lambda: await_bytes(v.at[:, pl.ds(0, 6)], r)

    def add_all(acc, v, w):
        total = dot_t(v[0].reshape(8 * R, 256), w[0]) + dot_t(v[1].reshape(8 * R, 256), w[1])
        acc[...] += total.reshape(8, R, 256)

    def reduce_start(p, s_ref, r_ref):
        r = sem()
        s_ref[...] = p[...].astype(BF)
        for i, (dx, dc) in enumerate(NEAR):
            other = colm(dx, dc)
            send(s_ref.at[other], r_ref.at[i], r, (z, other, l))

        def result():
            await_bytes(r_ref, r)
            total = p[c]
            for i in range(7):
                total = total + r_ref[i].astype(F32)
            return total

        return result

    a_recv = [sem(), sem()]

    def reduce_leaf_start(m, h):
        s_ref = s_a.at[m, h]
        s_ref[...] = p_a[m, h].astype(BF)
        slot = lax.rem(l - h + 4, 4)
        for k, (dx, dc) in enumerate(NEAR + [(0, 0)]):
            other = colm(dx, dc)
            if k < 7:
                send(s_ref.at[other], r_a.at[m, 4 * k + slot], a_recv[m], (z, other, h))
            else:
                there = (r_a.at[m, 27 + slot], (z, other, h))
                send_unless(l == h, s_ref.at[other], None, a_recv[m], there)

    def reduce_leaf_result(m):
        await_bytes(r_a.at[m], a_recv[m])
        total = p_a[m, l, c]
        for slot in range(31):
            total = total + r_a[m, slot].astype(F32)
        return total

    def spread_root(src, dst):
        r = sem()
        for d in (8, 7, 9, 6, 10, 5, 11, 4, 12, 3, 13, 2, 14, 1, 15):
            send(src, dst, r, (zed(d), ct, l))
        send_unless(ct == c, src, dst, r, (dst, (z, ct, l)))
        return lambda: await_bytes(v_z, r)

    def multiply_root(get, w, p):
        total = dot_t(get(0).reshape(128, 256), w[0]) + dot_t(get(1).reshape(128, 256), w[1])
        p[...] = total.reshape(8, 16, 256)

    lower_b = lambda k, h: b_leaf[k, pl.ds(R * h, R)].astype(F32)

    first_load()
    for h in range(H):
        yb[0, h] = solve(i_ll.at[0], lower_b(0, h))
    load_rest()
    for g in range(2):
        i_both[g] = lax.dot_general(
            i_ru[1, g],
            i_rl[1, g],
            (((1,), (0,)), ((), ())),
            preferred_element_type=F32,
            precision=lax.Precision.HIGHEST,
        )
    pl.semaphore_wait(barrier, greeted)

    def lower(h):
        far = spread_far(yb.at[0, h], v_y.at[0, h])
        yield
        far()
        near = spread_near(v_y.at[0, h])
        yield
        if h == 0:
            load_ll()
        near()
        add_all(p_y.at[h], v_y.at[0, h], w_ll)
        total = reduce_start(p_y.at[h], s_y.at[h], r_y.at[h])
        yield
        for m in range(2):
            add_all(p_a.at[m, h], v_y.at[0, h], w_cl.at[m, 0])
        yield
        yb[1, h] = solve(i_ll.at[1], lower_b(1, h) - total())
        far = spread_far(yb.at[1, h], v_y.at[1, h])
        yield
        far()
        near = spread_near(v_y.at[1, h])
        yield
        near()
        add_all(p_a.at[0, h], v_y.at[1, h], w_cl.at[0, 1])
        reduce_leaf_start(0, h)

    gathered = {}

    def gather_send(m):
        gathered[m] = [None] + [sem() for _ in range(3)]
        for d in (2, 1, 3):
            send(v_x.at[m, l], v_x.at[m, l], gathered[m][4 - d], (z, c, plane(d)))

    def gather_wait(m, t):
        if t:
            await_bytes(v_z, gathered[m][t])

    ro_recv = sem()

    def out_send(m):
        ro[m, l] = xb[m]
        for d in (2, 1, 3):
            send(xb.at[m], ro.at[m, l], ro_recv, (z, c, plane(d)))

    def root():
        rows = pl.ds(pl.multiple_of(l * 16, 16), 16)
        zb[0] = solve(i_rl.at[0], b_root[0, rows].astype(F32) - reduce_leaf_result(0))
        done = spread_root(zb.at[0], v_z.at[lax.rem(z, 2), c])
        for h in range(H):
            add_all(p_a.at[1, h], v_y.at[1, h], w_cl.at[1, 1])
            reduce_leaf_start(1, h)
        base1[...] = b_root[1, rows].astype(F32) - reduce_leaf_result(1)
        done()
        multiply_root(lambda b: v_z[b], w_rl, p_r.at[0])
        total = reduce_start(p_r.at[0], s_r.at[0], r_r.at[0])
        xb[1] = solve(i_both, base1[...] - total())
        done = spread_root(xb.at[1], v_x.at[1, l, lax.rem(z, 2), c])
        out_send(1)
        done()
        gather_send(1)
        multiply_root(lambda b: v_x[1, l, b], w_ru, p_r.at[1])
        total = reduce_start(p_r.at[1], s_r.at[1], r_r.at[1])
        xb[0] = solve(i_ru.at[0], zb[0].astype(F32) - total())
        done = spread_root(xb.at[0], v_x.at[0, l, lax.rem(z, 2), c])
        out_send(0)
        for t in TURNS:
            gather_wait(1, t)
            for k in (1, 0):
                add_all(p_w.at[k, t], v_x.at[1, plane(t)], w_cu.at[k, 1])
        done()
        gather_send(0)

    def upper(t):
        h = plane(t)
        rows = pl.ds(pl.multiple_of(h * R, R), R)
        gather_wait(0, t)
        add_all(p_w.at[1, t], v_x.at[0, h], w_cu.at[1, 0])
        total = reduce_start(p_w.at[1, t], s_w.at[1, t], r_w.at[1, t])
        yield
        add_all(p_w.at[0, t], v_x.at[0, h], w_cu.at[0, 0])
        yield
        wb[t] = solve(i_lu.at[1], yb[1, h].astype(F32) - total())
        far = spread_far(wb.at[t], v_w.at[t])
        leaf_out[0, 1, rows] = wb[t]
        yield
        far()
        near = spread_near(v_w.at[t])
        yield
        near()
        add_all(p_w.at[0, t], v_w.at[t], w_lu)
        total = reduce_start(p_w.at[0, t], s_w.at[0, t], r_w.at[0, t])
        yield
        leaf_out[0, 0, rows] = solve(i_lu.at[0], yb[0, h].astype(F32) - total())

    def in_turn(chains):
        chains = list(chains)
        while chains:
            chains = [chain for chain in chains if next(chain, chain) is not chain]

    in_turn([lower(h) for h in range(H)])
    root()
    chains = [upper(t) for t in range(4)]
    for t in ORDER:
        next(chains[t], None)
    await_bytes(bytes_of.at[pl.ds(0, 6)], ro_recv)
    for m in range(2):
        root_out[m] = ro[m].reshape(64, 256)
    await_bytes(bytes_of.at[pl.ds(0, units[0])], gone)


def on_device(*args):
    vmem = pltpu.VMEM
    scratch = [
        vmem((2, 64, 256), BF),
        vmem((2, 64, 256), BF),
        vmem((2, 256, 256), BF),
        vmem((2, 2, 2, 256, 256), BF),
        vmem((2, 256, 256), BF),
        vmem((2, 256, 256), BF),
        vmem((2, 2, 2, 256, 256), BF),
        vmem((2, 256, 256), BF),
        vmem((2, 2, 128, 128), F32),
        vmem((2, 2, 128, 128), F32),
        vmem((2, 2, 128, 128), F32),
        vmem((2, 2, 128, 128), F32),
        vmem((2, H, R, 256), BF),
        vmem((H, R, 256), BF),
        vmem((2, 16, 256), BF),
        vmem((2, 16, 256), BF),
        vmem((16, 256), F32),
        vmem((2, H, 2, 8, R, 256), BF),
        vmem((H, 2, 8, R, 256), BF),
        vmem((2, 8, 16, 256), BF),
        vmem((2, H, 2, 8, R, 256), BF),
        vmem((H, 8, R, 256), F32),
        vmem((2, H, 8, R, 256), F32),
        vmem((2, H, 8, R, 256), F32),
        vmem((2, 8, 16, 256), F32),
        vmem((H, 8, R, 256), BF),
        vmem((2, H, 8, R, 256), BF),
        vmem((2, H, 8, R, 256), BF),
        vmem((2, 8, 16, 256), BF),
        vmem((H, 7, R, 256), BF),
        vmem((2, 31, 16, 256), BF),
        vmem((2, H, 7, R, 256), BF),
        vmem((2, 7, 16, 256), BF),
        vmem((2, 4, 16, 256), BF),
        vmem((24, 16, 256), BF),
        vmem((1024, 16, 256), BF),
        vmem((2, 128, 128), F32),
        pltpu.SemaphoreType.DMA((N_SEM,)),
    ]
    return pl.pallas_call(
        kernel,
        out_shape=(
            jax.ShapeDtypeStruct((1, 2, 64, 256), BF),
            jax.ShapeDtypeStruct((2, 64, 256), BF),
        ),
        in_specs=[pl.BlockSpec(memory_space=pl.ANY)] * 12,
        out_specs=(pl.BlockSpec(memory_space=pltpu.VMEM),) * 2,
        scratch_shapes=scratch,
        compiler_params=pltpu.CompilerParams(
            collective_id=0, has_side_effects=True, vmem_limit_bytes=63 * 2**20
        ),
    )(*args)


def solution(mesh):
    placed = (
        P("leaf", None, "col", "row"),
        P(None, "col", "row"),
        P("leaf", None, "row", "col"),
        P("leaf", None, None, "row", "col"),
        P(None, "row", "col"),
        P("leaf", None, "row", "col"),
        P("leaf", None, None, "row", "col"),
        P(None, "row", "col"),
        P("leaf", None, "row", None, None),
        P(None, "row", None, None),
        P("leaf", None, "row", None, None),
        P(None, "row", None, None),
    )
    return jax.shard_map(
        on_device,
        mesh=mesh,
        in_specs=placed,
        out_specs=(P("leaf", None, "col", "row"), P(None, "col", "row")),
        check_vma=False,
    )
```

```python
import jax
import jax.numpy as jnp
from jax import lax
from jax.experimental import pallas as pl
from jax.experimental.pallas import tpu as pltpu
from jax.sharding import PartitionSpec as P

MESH = pl.DeviceIdType.MESH
H = 4
TURNS = (0, 1, 3, 2)
ORDER = (0, 0, 0, 1, 3, 2, 1, 3, 2, 0, 1, 3, 2, 0, 1, 3, 2, 0, 1, 3, 2, 1, 3, 2)
R = 64 // H
BF = jnp.bfloat16
F32 = jnp.float32
NEAR = [(2, 0), (2, 1), (1, 0), (1, 1), (3, 0), (3, 1), (0, 1)]
N_SEM = 57


def dot_t(a, b):
    return lax.dot_general(a, b, (((1,), (1,)), ((), ())), preferred_element_type=F32)


def solve(inverse, right):
    parts = []
    for s in range(2):
        parts.append(
            lax.dot_general(
                right[:, 128 * s : 128 * (s + 1)],
                inverse[s],
                (((1,), (1,)), ((), ())),
                preferred_element_type=F32,
                precision=lax.Precision.HIGHEST,
            )
        )
    return jnp.concatenate(parts, axis=1).astype(BF)


def kernel(
    leaf_rhs,
    root_rhs,
    leaf_lower,
    coupling_lower,
    root_lower,
    leaf_upper,
    coupling_upper,
    root_upper,
    leaf_lower_inv,
    root_lower_inv,
    leaf_upper_inv,
    root_upper_inv,
    leaf_out,
    root_out,
    b_leaf,
    b_root,
    w_ll,
    w_cl,
    w_rl,
    w_lu,
    w_cu,
    w_ru,
    i_ll,
    i_rl,
    i_lu,
    i_ru,
    yb,
    wb,
    zb,
    xb,
    base1,
    v_y,
    v_w,
    v_z,
    v_x,
    p_y,
    p_a,
    p_w,
    p_r,
    s_y,
    s_a,
    s_w,
    s_r,
    r_y,
    r_a,
    r_w,
    r_r,
    ro,
    spare,
    bytes_of,
    i_both,
    sems,
):
    z = lax.axis_index("row")
    c = lax.axis_index("col")
    l = lax.axis_index("leaf")
    x = lax.div(c, 2)
    core = lax.rem(c, 2)
    ct = lax.div(z, 2)
    taken = [0]

    def sem():
        taken[0] += 1
        return sems.at[taken[0] - 1]

    def zed(d):
        return lax.rem(z + (d + 32), 16)

    def plane(d):
        return lax.rem(l + (d + 8), 4)

    def colm(dx, dc):
        return lax.rem(x + (dx + 4), 4) * 2 + lax.rem(core + dc, 2)

    def await_bytes(ref, s):
        pltpu.make_async_copy(ref, ref, s).wait()

    gone = sem()
    units = [0, 0]

    def size(ref):
        total = 1
        for n in ref.shape:
            total *= n
        return total // 4096

    def send(src, dst, recv_sem, where):
        units[0] += size(src)
        pltpu.make_async_remote_copy(
            src_ref=src, dst_ref=dst, send_sem=gone, recv_sem=recv_sem, device_id=where, device_id_type=MESH
        ).start()

    def send_unless(me, src, dst, recv_sem, where):
        unused = spare.at[units[1]]
        units[1] += 1

        @pl.when(me)
        def _():
            if dst is not None:
                pltpu.make_async_copy(src, dst, recv_sem).start()
            pltpu.make_async_copy(src, unused, gone).start()

        @pl.when(jnp.logical_not(me))
        def _():
            send(src, where[0], recv_sem, where[1])

    def load(pairs):
        s, total = sem(), 0
        for src, dst in pairs:
            pltpu.make_async_copy(src, dst, s).start()
            total += size(dst) * (2 if dst.dtype == F32 else 1)
        return lambda: await_bytes(bytes_of.at[pl.ds(0, total)], s)

    def halves(src, dst):
        return [(src.at[:, pl.ds(256 * b, 256)], dst.at[b]) for b in range(2)]

    barrier = pltpu.get_barrier_semaphore()

    def greet(where):
        pl.semaphore_signal(barrier, inc=1, device_id=where, device_id_type=MESH)

    greeted = 0
    for b in range(2):
        for k in range(8):
            greet((2 * c + b, k, l))
            greeted += 1
    for dy in range(4):
        for dx, dc in NEAR + [(0, 0)]:
            if (dy, dx, dc) != (0, 0, 0):
                greet((z, colm(dx, dc), plane(dy)))
                greeted += 1
    for d in (-2, -1, 1, 2):
        greet((zed(d), c, l))
        greeted += 1

    first_load = load([(leaf_rhs.at[0], b_leaf), (leaf_lower_inv.at[0], i_ll)])
    load_ll = load(halves(leaf_lower.at[0, 0], w_ll))
    pairs = [(root_rhs, b_root), (root_lower_inv, i_rl), (leaf_upper_inv.at[0], i_lu), (root_upper_inv, i_ru)]
    for m in range(2):
        for j in range(2):
            pairs += halves(coupling_lower.at[0, m, j], w_cl.at[m, j])
            pairs += halves(coupling_upper.at[0, m, j], w_cu.at[m, j])
    pairs += halves(root_lower.at[0], w_rl)
    pairs += halves(leaf_upper.at[0, 0], w_lu)
    pairs += halves(root_upper.at[0], w_ru)
    load_rest = load(pairs)

    p_y[...] = jnp.zeros_like(p_y)
    p_a[...] = jnp.zeros_like(p_a)
    p_w[...] = jnp.zeros_like(p_w)

    def spread_far(src, v):
        r = sem()
        off = 1 + lax.rem(z, 2) + lax.div(c, 4)
        dst = v.at[lax.rem(z, 2), c]
        for i in (2, 1, 3, 0):
            send(src, dst, r, (zed(off + 4 * i), ct, l))
        return lambda: await_bytes(v.at[0, pl.ds(0, 4)], r)

    def spread_near(v):
        j = lax.rem(z - 2 * c + 31, 4)
        b, first = lax.div(j, 2), lax.rem(j, 2) * 4
        block = v.at[b, pl.ds(first, 4)]
        parts = [v.at[b, pl.ds(first, 2)], v.at[b, pl.ds(first + 2, 2)]]
        r = sem()
        send(parts[0], parts[0], r, (zed(2), c, l))
        send(parts[1], parts[1], r, (zed(-2), c, l))
        send(block, block, r, (zed(1), c, l))
        send(block, block, r, (zed(-1), c, l))
        return lambda: await_bytes(v.at[:, pl.ds(0, 6)], r)

    def add_all(acc, v, w):
        total = dot_t(v[0].reshape(8 * R, 256), w[0]) + dot_t(v[1].reshape(8 * R, 256), w[1])
        acc[...] += total.reshape(8, R, 256)

    def reduce_start(p, s_ref, r_ref):
        r = sem()
        s_ref[...] = p[...].astype(BF)
        for i, (dx, dc) in enumerate(NEAR):
            other = colm(dx, dc)
            send(s_ref.at[other], r_ref.at[i], r, (z, other, l))

        def result():
            await_bytes(r_ref, r)
            total = p[c]
            for i in range(7):
                total = total + r_ref[i].astype(F32)
            return total

        return result

    a_recv = [sem(), sem()]

    def reduce_leaf_start(m, h):
        s_ref = s_a.at[m, h]
        s_ref[...] = p_a[m, h].astype(BF)
        slot = lax.rem(l - h + 4, 4)
        for k, (dx, dc) in enumerate(NEAR + [(0, 0)]):
            other = colm(dx, dc)
            if k < 7:
                send(s_ref.at[other], r_a.at[m, 4 * k + slot], a_recv[m], (z, other, h))
            else:
                there = (r_a.at[m, 27 + slot], (z, other, h))
                send_unless(l == h, s_ref.at[other], None, a_recv[m], there)

    def reduce_leaf_result(m):
        await_bytes(r_a.at[m], a_recv[m])
        total = p_a[m, l, c]
        for slot in range(31):
            total = total + r_a[m, slot].astype(F32)
        return total

    def spread_root(src, dst):
        first = taken[0]
        taken[0] += 2
        r = sems.at[first + lax.rem(z, 2)]
        for d in (8, 7, 9, 6, 10, 5, 11, 4, 12, 3, 13, 2, 14, 1, 15):
            send(src, dst, r, (zed(d), ct, l))
        send_unless(ct == c, src, dst, r, (dst, (z, ct, l)))
        return lambda b: await_bytes(v_z.at[0], sems.at[first + b])

    def multiply_root(get, w, p):
        total = dot_t(get(0).reshape(128, 256), w[0]) + dot_t(get(1).reshape(128, 256), w[1])
        p[...] = total.reshape(8, 16, 256)

    lower_b = lambda k, h: b_leaf[k, pl.ds(R * h, R)].astype(F32)

    first_load()
    for h in range(H):
        yb[0, h] = solve(i_ll.at[0], lower_b(0, h))
    load_rest()
    for g in range(2):
        i_both[g] = lax.dot_general(
            i_ru[1, g],
            i_rl[1, g],
            (((1,), (0,)), ((), ())),
            preferred_element_type=F32,
            precision=lax.Precision.HIGHEST,
        )
    pl.semaphore_wait(barrier, greeted)

    def lower(h):
        far = spread_far(yb.at[0, h], v_y.at[0, h])
        yield
        far()
        near = spread_near(v_y.at[0, h])
        yield
        if h == 0:
            load_ll()
        near()
        add_all(p_y.at[h], v_y.at[0, h], w_ll)
        total = reduce_start(p_y.at[h], s_y.at[h], r_y.at[h])
        yield
        for m in range(2):
            add_all(p_a.at[m, h], v_y.at[0, h], w_cl.at[m, 0])
        yield
        yb[1, h] = solve(i_ll.at[1], lower_b(1, h) - total())
        far = spread_far(yb.at[1, h], v_y.at[1, h])
        yield
        far()
        near = spread_near(v_y.at[1, h])
        yield
        near()
        add_all(p_a.at[0, h], v_y.at[1, h], w_cl.at[0, 1])
        reduce_leaf_start(0, h)

    gathered = {}

    close = (lax.rem(z - 2 * c + 31, 16) < 8).astype(jnp.int32)

    def gather_send(m, done):
        gathered[m] = [None] + [sem() for _ in range(3)]
        for b in (close, 1 - close):
            done(b)
            part = v_x.at[m, l, b]
            for d in (2, 1, 3):
                send(part, part, gathered[m][4 - d], (z, c, plane(d)))

    def gather_wait(m, t):
        if t:
            await_bytes(v_z, gathered[m][t])

    ro_recv = sem()

    def out_send(m):
        ro[m, l] = xb[m]
        for d in (2, 1, 3):
            send(xb.at[m], ro.at[m, l], ro_recv, (z, c, plane(d)))

    def root():
        rows = pl.ds(pl.multiple_of(l * 16, 16), 16)
        zb[0] = solve(i_rl.at[0], b_root[0, rows].astype(F32) - reduce_leaf_result(0))
        done = spread_root(zb.at[0], v_z.at[lax.rem(z, 2), c])
        for h in range(H):
            add_all(p_a.at[1, h], v_y.at[1, h], w_cl.at[1, 1])
            reduce_leaf_start(1, h)
        base1[...] = b_root[1, rows].astype(F32) - reduce_leaf_result(1)
        done(0)
        done(1)
        multiply_root(lambda b: v_z[b], w_rl, p_r.at[0])
        total = reduce_start(p_r.at[0], s_r.at[0], r_r.at[0])
        xb[1] = solve(i_both, base1[...] - total())
        done = spread_root(xb.at[1], v_x.at[1, l, lax.rem(z, 2), c])
        out_send(1)
        gather_send(1, done)
        multiply_root(lambda b: v_x[1, l, b], w_ru, p_r.at[1])
        total = reduce_start(p_r.at[1], s_r.at[1], r_r.at[1])
        xb[0] = solve(i_ru.at[0], zb[0].astype(F32) - total())
        done = spread_root(xb.at[0], v_x.at[0, l, lax.rem(z, 2), c])
        out_send(0)
        for t in TURNS:
            gather_wait(1, t)
            for k in (1, 0):
                add_all(p_w.at[k, t], v_x.at[1, plane(t)], w_cu.at[k, 1])
        gather_send(0, done)

    def upper(t):
        h = plane(t)
        rows = pl.ds(pl.multiple_of(h * R, R), R)
        gather_wait(0, t)
        add_all(p_w.at[1, t], v_x.at[0, h], w_cu.at[1, 0])
        total = reduce_start(p_w.at[1, t], s_w.at[1, t], r_w.at[1, t])
        yield
        add_all(p_w.at[0, t], v_x.at[0, h], w_cu.at[0, 0])
        yield
        wb[t] = solve(i_lu.at[1], yb[1, h].astype(F32) - total())
        far = spread_far(wb.at[t], v_w.at[t])
        leaf_out[0, 1, rows] = wb[t]
        yield
        far()
        near = spread_near(v_w.at[t])
        yield
        near()
        add_all(p_w.at[0, t], v_w.at[t], w_lu)
        total = reduce_start(p_w.at[0, t], s_w.at[0, t], r_w.at[0, t])
        yield
        leaf_out[0, 0, rows] = solve(i_lu.at[0], yb[0, h].astype(F32) - total())

    def in_turn(chains):
        chains = list(chains)
        while chains:
            chains = [chain for chain in chains if next(chain, chain) is not chain]

    in_turn([lower(h) for h in range(H)])
    root()
    chains = [upper(t) for t in range(4)]
    for t in ORDER:
        next(chains[t], None)
    await_bytes(bytes_of.at[pl.ds(0, 6)], ro_recv)
    for m in range(2):
        root_out[m] = ro[m].reshape(64, 256)
    await_bytes(bytes_of.at[pl.ds(0, units[0])], gone)


def on_device(*args):
    vmem = pltpu.VMEM
    scratch = [
        vmem((2, 64, 256), BF),
        vmem((2, 64, 256), BF),
        vmem((2, 256, 256), BF),
        vmem((2, 2, 2, 256, 256), BF),
        vmem((2, 256, 256), BF),
        vmem((2, 256, 256), BF),
        vmem((2, 2, 2, 256, 256), BF),
        vmem((2, 256, 256), BF),
        vmem((2, 2, 128, 128), F32),
        vmem((2, 2, 128, 128), F32),
        vmem((2, 2, 128, 128), F32),
        vmem((2, 2, 128, 128), F32),
        vmem((2, H, R, 256), BF),
        vmem((H, R, 256), BF),
        vmem((2, 16, 256), BF),
        vmem((2, 16, 256), BF),
        vmem((16, 256), F32),
        vmem((2, H, 2, 8, R, 256), BF),
        vmem((H, 2, 8, R, 256), BF),
        vmem((2, 8, 16, 256), BF),
        vmem((2, H, 2, 8, R, 256), BF),
        vmem((H, 8, R, 256), F32),
        vmem((2, H, 8, R, 256), F32),
        vmem((2, H, 8, R, 256), F32),
        vmem((2, 8, 16, 256), F32),
        vmem((H, 8, R, 256), BF),
        vmem((2, H, 8, R, 256), BF),
        vmem((2, H, 8, R, 256), BF),
        vmem((2, 8, 16, 256), BF),
        vmem((H, 7, R, 256), BF),
        vmem((2, 31, 16, 256), BF),
        vmem((2, H, 7, R, 256), BF),
        vmem((2, 7, 16, 256), BF),
        vmem((2, 4, 16, 256), BF),
        vmem((24, 16, 256), BF),
        vmem((1024, 16, 256), BF),
        vmem((2, 128, 128), F32),
        pltpu.SemaphoreType.DMA((N_SEM,)),
    ]
    return pl.pallas_call(
        kernel,
        out_shape=(
            jax.ShapeDtypeStruct((1, 2, 64, 256), BF),
            jax.ShapeDtypeStruct((2, 64, 256), BF),
        ),
        in_specs=[pl.BlockSpec(memory_space=pl.ANY)] * 12,
        out_specs=(pl.BlockSpec(memory_space=pltpu.VMEM),) * 2,
        scratch_shapes=scratch,
        compiler_params=pltpu.CompilerParams(
            collective_id=0, has_side_effects=True, vmem_limit_bytes=63 * 2**20
        ),
    )(*args)


def solution(mesh):
    placed = (
        P("leaf", None, "col", "row"),
        P(None, "col", "row"),
        P("leaf", None, "row", "col"),
        P("leaf", None, None, "row", "col"),
        P(None, "row", "col"),
        P("leaf", None, "row", "col"),
        P("leaf", None, None, "row", "col"),
        P(None, "row", "col"),
        P("leaf", None, "row", None, None),
        P(None, "row", None, None),
        P("leaf", None, "row", None, None),
        P(None, "row", None, None),
    )
    return jax.shard_map(
        on_device,
        mesh=mesh,
        in_specs=placed,
        out_specs=(P("leaf", None, "col", "row"), P(None, "col", "row")),
        check_vma=False,
    )
```
